256 devices in a mesh: ka: 8 (over y, x_hi), ta: 32 (over x_lo, z, core).
Axes of the slice: x: 4 (x_hi: 2, x_lo: 2; x = x_hi * 2 + x_lo), y: 4, z: 8, core: 2. Of those that a mesh axis runs over, the one named last changes fastest.
Arguments:
- green_time: bfloat16 [2, 144, 2048, 128], P(None, 'ka', 'ta'), may hold values from -6 to 6
- screened_time: bfloat16 [2, 144, 2048, 128], P(None, 'ka', 'ta'), may hold values from -0.5 to 0.5
- panel_orbitals: bfloat16 [2, 144, 128, 128], P(None, 'ka'), may hold values from -0.1796875 to 0.1796875
- column_orbitals: bfloat16 [2, 144, 2048, 128], P(None, 'ka', 'ta'), may hold values from -0.1796875 to 0.1796875
Outputs:
- band_sigma: float32 [2, 2, 144, 128, 128], P(None, None, 'ka', None, 'ta')
The draws below stay inside these ranges and needn't reach their ends.
All inputs are finite; a program needn't handle non-finite values.
Results may differ from the reference program's by a relative error of at most 0.0049.
Values may be sent and summed in bfloat16 or wider, within the bound.
A program may use at most 64 MiB of HBM per device.

```python
import jax
import jax.numpy as jnp
from jax import lax

LA = 6
LC = 4
NK = 144
MU = 128
NU = 2048
NB = 128
NT = 2


def block_levels(rng, shape, cuts, smallest, largest):
    factor_of, own = 1.0, jax.random.fold_in(rng, 6)
    for dim, shards_of in cuts:
        draws = jnp.exp(jax.random.uniform(jax.random.fold_in(own, dim), (shards_of,), jnp.float32, smallest / len(cuts), largest / len(cuts)))
        factor_of = factor_of * jnp.repeat(draws, shape[dim] // shards_of).reshape([-1 if axis == dim else 1 for axis in range(len(shape))])
    return factor_of


def normal_values(key, extent, deviation, most, shards=(), kind=jnp.bfloat16):
    gain = block_levels(key, extent, shards, -0.22, 0.18) if shards else 1.0
    entries = jax.random.normal(key, extent, jnp.float32) * deviation * gain
    return jnp.minimum(jnp.maximum(entries, -most), most).astype(kind)


def setup_inputs(seed: int = 0) -> dict:
    splits = jax.random.split(jax.random.key(seed), 5)
    green_time = normal_values(splits[0], (NT, NK, NU, MU), 1.0, 6.0, ((1, 8), (2, 32)))
    screened_time = normal_values(splits[1], (NT, NK, NU, MU), 0.083, 0.5, ((1, 8), (2, 32)))
    panel_orbitals = normal_values(splits[2], (2, NK, MU, NB), 0.03, 0.1796875, ((1, 8),))
    column_orbitals = normal_values(splits[3], (2, NK, NU, NB), 0.03, 0.1796875, ((1, 8), (2, 32)))
    return {"green_time": green_time, "screened_time": screened_time, "panel_orbitals": panel_orbitals, "column_orbitals": column_orbitals}


def lattice_table():
    cells = jnp.arange(NK, dtype=jnp.int32)
    first = cells // (LA * LC)
    second = (cells // LC) % LA
    third = cells % LC
    outer = (first[:, None] * first[None, :] + second[:, None] * second[None, :]) % LA
    inner = (third[:, None] * third[None, :]) % LC
    turns = (outer * LC + inner * LA) % (LA * LC)
    angle = turns.astype(jnp.float32) * (2.0 * jnp.pi / (LA * LC))
    return jnp.stack([jnp.cos(angle), -jnp.sin(angle)])


def reference(green_time, screened_time, panel_orbitals, column_orbitals):
    table = lattice_table()
    panel = panel_orbitals.astype(jnp.float32)
    column = column_orbitals.astype(jnp.float32)

    def one_time(pair):
        green, screened = pair
        product = (green.astype(jnp.float32) * screened.astype(jnp.float32)).astype(jnp.bfloat16)
        spectral = jnp.einsum("ckr,rnm->cknm", table, product.astype(jnp.float32), precision=lax.Precision.HIGHEST).astype(jnp.bfloat16)
        s_real = spectral[0].astype(jnp.float32)
        s_imag = spectral[1].astype(jnp.float32)
        h_real = jnp.einsum("kmi,knm->kni", panel[0], s_real) + jnp.einsum("kmi,knm->kni", panel[1], s_imag)
        h_imag = jnp.einsum("kmi,knm->kni", panel[0], s_imag) - jnp.einsum("kmi,knm->kni", panel[1], s_real)
        half = jnp.stack([h_real, h_imag]).astype(jnp.bfloat16).astype(jnp.float32)
        z_real = jnp.einsum("kni,knj->kij", half[0], column[0]) - jnp.einsum("kni,knj->kij", half[1], column[1])
        z_imag = jnp.einsum("kni,knj->kij", half[0], column[1]) + jnp.einsum("kni,knj->kij", half[1], column[0])
        return jnp.stack([z_real, z_imag])

    return lax.map(one_time, (green_time, screened_time))
```

```python
import jax
import jax.numpy as jnp
from jax import lax
from jax.experimental import pallas as pl
from jax.experimental.pallas import tpu as pltpu
from jax.sharding import PartitionSpec as P

MESH = pl.DeviceIdType.MESH
BF = jnp.bfloat16
F32 = jnp.float32
NY, NX, NZ = 4, 4, 8
NA = 8
LA, LC = 6, 4
NK = 144
KB = 18
KH = 9
NCH = 3
KC = KH // NCH
SUB = 16
HALF_SQRT3 = 0.8660254037844386


def real_dft6(x):
    e0, e1, e2 = x[0] + x[3], x[1] + x[4], x[2] + x[5]
    o0, o1, o2 = x[0] - x[3], x[1] - x[4], x[2] - x[5]
    es = e1 + e2
    od = o1 - o2
    x1 = (o0 + 0.5 * od, -HALF_SQRT3 * (o1 + o2))
    x2 = (e0 - 0.5 * es, -HALF_SQRT3 * (e1 - e2))
    return e0 + es, o0 - od, x1, x2


def complex_dft6(re, im):
    a0, a3, a1, a2 = real_dft6(re)
    b0, b3, b1, b2 = real_dft6(im)
    return (
        (a0, b0),
        (a1[0] - b1[1], a1[1] + b1[0]),
        (a2[0] - b2[1], a2[1] + b2[0]),
        (a3, b3),
        (a2[0] + b2[1], b2[0] - a2[1]),
        (a1[0] + b1[1], b1[0] - a1[1]),
    )


def lattice_dft(cells, stage, spectral):
    def inner(r1, carry):
        block = cells[pl.ds(r1 * 24, 24)].astype(F32)
        zero, two, one_re, one_im = [], [], [], []
        for r2 in range(LA):
            x0, x1, x2, x3 = (block[4 * r2 + j] for j in range(LC))
            s02, s13 = x0 + x2, x1 + x3
            zero.append(s02 + s13)
            two.append(s02 - s13)
            one_re.append(x0 - x2)
            one_im.append(x3 - x1)
        for base, values in ((0, zero), (6, two)):
            v0, v3, v1, v2 = real_dft6(values)
            for slot, value in enumerate((v0, v3, v1[0], v1[1], v2[0], v2[1])):
                stage[r1, base + slot] = value
        for k2, pair in enumerate(complex_dft6(one_re, one_im)):
            stage[r1, 12 + 2 * k2] = pair[0]
            stage[r1, 13 + 2 * k2] = pair[1]
        return carry

    lax.fori_loop(0, LA, inner, 0)

    def put(k, re, im):
        spectral[0, k] = re.astype(BF)
        spectral[1, k] = im.astype(BF)

    def outer_complex(slot, k2, k3):
        re = [stage[r1, slot] for r1 in range(LA)]
        im = [stage[r1, slot + 1] for r1 in range(LA)]
        there = (LA - k2) % LA * LC + (LC - k3) % LC
        for k1, pair in enumerate(complex_dft6(re, im)):
            put(k1 * 24 + k2 * LC + k3, pair[0], pair[1])
            put((LA - k1) % LA * 24 + there, pair[0], -pair[1])

    def third_one(k2, carry):
        outer_complex(12 + 2 * k2, k2, 1)
        return carry

    lax.fori_loop(0, LA, third_one, 0)

    def third_even(i, carry):
        outer_complex(6 * (i // 2) + 2 + 2 * (i % 2), 1 + i % 2, 2 * (i // 2))
        return carry

    lax.fori_loop(0, 4, third_even, 0)

    def all_real(i, carry):
        k2, k3 = 3 * (i % 2), 2 * (i // 2)
        slot = 6 * (i // 2) + i % 2
        x0, x3, x1, x2 = real_dft6([stage[r1, slot] for r1 in range(LA)])
        base = k2 * LC + k3
        none = jnp.zeros_like(x0)
        put(base, x0, none)
        put(24 + base, x1[0], x1[1])
        put(48 + base, x2[0], x2[1])
        put(72 + base, x3, none)
        put(96 + base, x2[0], -x2[1])
        put(120 + base, x1[0], -x1[1])
        return carry

    lax.fori_loop(0, 4, all_real, 0)


def placing_tables():
    row = lax.broadcasted_iota(jnp.int32, (256, 256), 0)
    lane = lax.broadcasted_iota(jnp.int32, (256, 256), 1)
    j = ((row >> 4) & 1) * 64 + (row >> 5) * 8 + ((row >> 3) & 1) * 4 + (row & 3)
    part = (row >> 2) & 1
    first = jnp.where(lane == part * 128 + j, 1.0, 0.0)
    sign = jnp.where(part == 0, -1.0, 1.0)
    second = jnp.where(lane == (1 - part) * 128 + j, sign, 0.0)
    return first.astype(BF), second.astype(BF)


def kernel(
    green, screened, panel, column, out,
    g_buf, w_buf, product, cells, stage, spectral, sigma, pan, cols, placing, lhs, bands, to_send, received, quarter,
    load_sem, col_local, col_send, col_recv, p1_send, p1_recv, p2_send, p2_recv, r_send, r_recv, f_send, f_recv,
):
    ka = lax.axis_index("ka")
    ta = lax.axis_index("ta")
    y, xh = ka // 2, ka % 2
    xl, z, core = ta // (2 * NZ), ta // 2 % NZ, ta % 2
    x = 2 * xh + xl

    def device(y_, x_, z_, core_):
        return (y_ * 2 + x_ // 2, (x_ % 2 * NZ + z_) * 2 + core_)

    loads = [
        pltpu.make_async_copy(green, g_buf, load_sem.at[0]),
        pltpu.make_async_copy(screened, w_buf, load_sem.at[1]),
        pltpu.make_async_copy(panel.at[:, pl.ds(KH * xl, KH)], pan, load_sem.at[2]),
        pltpu.make_async_copy(column.at[:, pl.ds(KH * xl, KH)], cols.at[xl, core], col_local),
    ]
    for load in loads:
        load.start()

    barrier = pltpu.get_barrier_semaphore()

    def greet_plane(d, carry):
        there = device((y + d // 8) % NY, (x + d // 2 % NX) % NX, z, (core + d % 2) % 2)
        pl.semaphore_signal(barrier, inc=1, device_id=there, device_id_type=MESH)
        return carry

    lax.fori_loop(1, 32, greet_plane, 0)

    def greet_z(d, carry):
        pl.semaphore_signal(barrier, inc=1, device_id=device(y, x, (z + d) % NZ, core), device_id_type=MESH)
        return carry

    lax.fori_loop(1, NZ, greet_z, 0)

    loads[0].wait()
    loads[1].wait()

    def multiply(r, carry):
        for t in range(2):
            product[t, r] = (g_buf[t, r].astype(F32) * w_buf[t, r].astype(F32)).astype(BF)
        return carry

    lax.fori_loop(0, KB, multiply, 0)
    pl.semaphore_wait(barrier, 31 + NZ - 1)

    def send_cells(i, carry):
        sub, t = i // 2, i % 2
        there = 4 * core + sub
        pltpu.make_async_remote_copy(
            src_ref=product.at[t, :, pl.ds(pl.multiple_of(sub * SUB, SUB), SUB)],
            dst_ref=cells.at[pl.ds(ka * KB, KB)],
            send_sem=p1_send,
            recv_sem=p1_recv,
            device_id=device(there // 2, 2 * (there % 2) + 1 - xl, z, t),
            device_id_type=MESH,
        ).start()
        return carry

    lax.fori_loop(0, 8, send_cells, 0)

    to_core = pltpu.make_async_remote_copy(
        src_ref=column.at[:, pl.ds(KH * xl, KH)],
        dst_ref=cols.at[xl, core],
        send_sem=col_send.at[0],
        recv_sem=col_recv.at[0],
        device_id=device(y, x, z, 1 - core),
        device_id_type=MESH,
    )
    to_x = pltpu.make_async_remote_copy(
        src_ref=column.at[:, pl.ds(KH * (1 - xl), KH)],
        dst_ref=cols.at[xl, core],
        send_sem=col_send.at[1],
        recv_sem=col_recv.at[1],
        device_id=device(y, 2 * xh + 1 - xl, z, core),
        device_id_type=MESH,
    )
    forward = pltpu.make_async_remote_copy(
        src_ref=cols.at[1 - xl, core],
        dst_ref=cols.at[1 - xl, core],
        send_sem=col_send.at[2],
        recv_sem=col_recv.at[2],
        device_id=device(y, x, z, 1 - core),
        device_id_type=MESH,
    )
    to_core.start()
    to_x.start()

    first, second = placing_tables()
    placing[0:256] = first
    placing[256:512] = second

    pltpu.make_async_copy(cells, cells, p1_recv).wait()
    lattice_dft(cells, stage, spectral)

    mine = (1 - xl) * NA + ka
    for chunk in range(NCH):
        own_k = (ka * 2 + xl) * KH + chunk * KC
        pltpu.make_async_copy(
            spectral.at[:, pl.ds(own_k, KC)], sigma.at[chunk, mine], p2_recv.at[chunk]
        ).start()

        def send_points(d, carry, chunk=chunk):
            y_, x_ = (y + d // NX) % NY, (x + d % NX) % NX
            k = (y_ * NX + x_) * KH + chunk * KC
            pltpu.make_async_remote_copy(
                src_ref=spectral.at[:, pl.ds(k, KC)],
                dst_ref=sigma.at[chunk, mine],
                send_sem=p2_send,
                recv_sem=p2_recv.at[chunk],
                device_id=device(y_, x_, z, core),
                device_id_type=MESH,
            ).start()
            return carry

        lax.fori_loop(1, NY * NX, send_points, 0)

    to_x.wait_recv()
    forward.start()
    loads[2].wait()
    loads[3].wait()
    to_core.wait_recv()
    forward.wait_recv()

    def place(k, carry):
        parts = [
            jnp.concatenate([cols[a, b, part, k] for a in range(2) for b in range(2)], axis=0)
            for part in range(2)
        ]
        both = jnp.concatenate(parts, axis=1)
        placed = lax.dot_general(
            placing[...], both, (((1,), (1,)), ((), ())), preferred_element_type=F32
        ).astype(BF)
        lhs[k] = jnp.concatenate([placed[0:256], placed[256:512]], axis=1)
        return carry

    lax.fori_loop(0, KH, place, 0)

    for chunk in range(NCH):
        pltpu.make_async_copy(sigma.at[chunk], sigma.at[chunk], p2_recv.at[chunk]).wait()

        def contract(kk, carry, chunk=chunk):
            k = chunk * KC + kk
            s = jnp.concatenate(
                [sigma[chunk, :, part, kk].reshape(256, 128) for part in range(2)], axis=1
            )
            p_re, p_im = pan[0, k], pan[1, k]
            weights = jnp.concatenate(
                [jnp.concatenate([p_re, -p_im], axis=1), jnp.concatenate([p_im, p_re], axis=1)], axis=0
            )
            half = jnp.dot(s, weights, preferred_element_type=F32).astype(BF)
            stacked = jnp.concatenate([half[:, 0:128], half[:, 128:256]], axis=0)
            band = jnp.dot(lhs[k], stacked, preferred_element_type=F32)
            bands[k] = band
            to_send[k] = band.astype(BF).reshape(NZ, 32, 128)
            return carry

        lax.fori_loop(0, KC, contract, 0)

        def send_bands(d, carry, chunk=chunk):
            z_ = (z + d) % NZ
            pltpu.make_async_remote_copy(
                src_ref=to_send.at[pl.ds(chunk * KC, KC), z_],
                dst_ref=received.at[chunk, z],
                send_sem=r_send,
                recv_sem=r_recv.at[chunk],
                device_id=device(y, x, z_, core),
                device_id_type=MESH,
            ).start()
            return carry

        lax.fori_loop(1, NZ, send_bands, 0)

    for chunk in range(NCH):
        some = received.at[chunk, pl.ds(0, NZ - 1)]
        pltpu.make_async_copy(some, some, r_recv.at[chunk]).wait()

        def add_up(kk, carry, chunk=chunk):
            k = chunk * KC + kk
            total = bands[k, pl.ds(pl.multiple_of(z * 32, 32), 32)]
            for d in range(1, NZ):
                total = total + received[chunk, (z + d) % NZ, kk].astype(F32)
            for g in range(4):
                quarter[g, k] = total[8 * g : 8 * g + 8]
            return carry

        lax.fori_loop(0, KC, add_up, 0)

    for d in range(1, 4):
        xl_, core_ = (xl + d // 2) % 2, (core + d % 2) % 2
        pltpu.make_async_remote_copy(
            src_ref=quarter.at[2 * xl_ + core_],
            dst_ref=out.at[core, pl.ds(KH * xl, KH)],
            send_sem=f_send,
            recv_sem=f_recv,
            device_id=device(y, 2 * xh + xl_, z, core_),
            device_id_type=MESH,
        ).start()
    out[core, pl.ds(KH * xl, KH)] = quarter[2 * xl + core]

    three = quarter.at[pl.ds(0, 3)]
    pltpu.make_async_copy(three, three, f_recv).wait()

    pltpu.make_async_copy(cells, cells, p1_send).wait()
    to_core.wait_send()
    to_x.wait_send()
    forward.wait_send()
    others = sigma.at[:, pl.ds(0, NY * NX - 1)]
    pltpu.make_async_copy(others, others, p2_send).wait()
    others = received.at[:, pl.ds(0, NZ - 1)]
    pltpu.make_async_copy(others, others, r_send).wait()
    pltpu.make_async_copy(three, three, f_send).wait()


def body(green, screened, panel, column):
    dma = pltpu.SemaphoreType.DMA
    bands = pl.pallas_call(
        kernel,
        out_shape=jax.ShapeDtypeStruct((2, KB, 8, 128), F32),
        in_specs=[pl.BlockSpec(memory_space=pltpu.HBM)] * 4,
        out_specs=pl.BlockSpec(memory_space=pltpu.VMEM),
        scratch_shapes=[
            pltpu.VMEM((2, KB, 64, 128), BF),
            pltpu.VMEM((2, KB, 64, 128), BF),
            pltpu.VMEM((2, KB, 64, 128), BF),
            pltpu.VMEM((NK, SUB, 128), BF),
            pltpu.VMEM((LA, 24, SUB, 128), F32),
            pltpu.VMEM((2, NK, SUB, 128), BF),
            pltpu.VMEM((NCH, 16, 2, KC, SUB, 128), BF),
            pltpu.VMEM((2, KH, 128, 128), BF),
            pltpu.VMEM((2, 2, 2, KH, 64, 128), BF),
            pltpu.VMEM((512, 256), BF),
            pltpu.VMEM((KH, 256, 512), BF),
            pltpu.VMEM((KH, 256, 128), F32),
            pltpu.VMEM((KH, NZ, 32, 128), BF),
            pltpu.VMEM((NCH, NZ, KC, 32, 128), BF),
            pltpu.VMEM((4, KH, 8, 128), F32),
            dma((3,)),
            dma,
            dma((3,)),
            dma((3,)),
            dma,
            dma,
            dma,
            dma((NCH,)),
            dma,
            dma((NCH,)),
            dma,
            dma,
        ],
        compiler_params=pltpu.CompilerParams(
            collective_id=0, has_side_effects=True, vmem_limit_bytes=60 * 1024 * 1024
        ),
    )(green, screened, panel, column)
    return jnp.transpose(bands.reshape(2, KB, 2, 4, 128), (0, 2, 1, 4, 3))


def solution(mesh):
    return jax.shard_map(
        body,
        mesh=mesh,
        in_specs=(
            P(None, "ka", "ta", None),
            P(None, "ka", "ta", None),
            P(None, "ka", None, None),
            P(None, "ka", "ta", None),
        ),
        out_specs=P(None, None, "ka", None, "ta"),
        check_vma=False,
    )
```

```python
import jax
import jax.numpy as jnp
from jax import lax
from jax.experimental import pallas as pl
from jax.experimental.pallas import tpu as pltpu
from jax.sharding import PartitionSpec as P

MESH = pl.DeviceIdType.MESH
BF = jnp.bfloat16
F32 = jnp.float32
NY, NX, NZ = 4, 4, 8
NA = 8
LA, LC = 6, 4
NK = 144
KB = 18
KH = 9
CHUNKS = (2, 2, 2, 1, 2)
STARTS = tuple(sum(CHUNKS[:i]) for i in range(len(CHUNKS)))
LAST = len(CHUNKS) - 1
EARLY = KH - CHUNKS[LAST]
AHEAD = 3
FAR_FIRST = sorted(
    ((dy, dx) for dy in range(NY) for dx in range(NX) if dy or dx),
    key=lambda d: -min(d[0], NY - d[0]) - min(d[1], NX - d[1]),
)
SUB = 16
HALF_SQRT3 = 0.8660254037844386


def real_dft6(x):
    e0, e1, e2 = x[0] + x[3], x[1] + x[4], x[2] + x[5]
    o0, o1, o2 = x[0] - x[3], x[1] - x[4], x[2] - x[5]
    es = e1 + e2
    od = o1 - o2
    x1 = (o0 + 0.5 * od, -HALF_SQRT3 * (o1 + o2))
    x2 = (e0 - 0.5 * es, -HALF_SQRT3 * (e1 - e2))
    return e0 + es, o0 - od, x1, x2


def complex_dft6(re, im):
    a0, a3, a1, a2 = real_dft6(re)
    b0, b3, b1, b2 = real_dft6(im)
    return (
        (a0, b0),
        (a1[0] - b1[1], a1[1] + b1[0]),
        (a2[0] - b2[1], a2[1] + b2[0]),
        (a3, b3),
        (a2[0] + b2[1], b2[0] - a2[1]),
        (a1[0] + b1[1], b1[0] - a1[1]),
    )


def lattice_dft(cells, stage, spectral):
    def inner(r1, carry):
        block = cells[pl.ds(r1 * 24, 24)].astype(F32)
        zero, two, one_re, one_im = [], [], [], []
        for r2 in range(LA):
            x0, x1, x2, x3 = (block[4 * r2 + j] for j in range(LC))
            s02, s13 = x0 + x2, x1 + x3
            zero.append(s02 + s13)
            two.append(s02 - s13)
            one_re.append(x0 - x2)
            one_im.append(x3 - x1)
        for base, values in ((0, zero), (6, two)):
            v0, v3, v1, v2 = real_dft6(values)
            for slot, value in enumerate((v0, v3, v1[0], v1[1], v2[0], v2[1])):
                stage[r1, base + slot] = value
        for k2, pair in enumerate(complex_dft6(one_re, one_im)):
            stage[r1, 12 + 2 * k2] = pair[0]
            stage[r1, 13 + 2 * k2] = pair[1]
        return carry

    lax.fori_loop(0, LA, inner, 0)

    def put(k, re, im):
        spectral[0, k] = re.astype(BF)
        spectral[1, k] = im.astype(BF)

    def outer_complex(slot, k2, k3):
        re = [stage[r1, slot] for r1 in range(LA)]
        im = [stage[r1, slot + 1] for r1 in range(LA)]
        there = (LA - k2) % LA * LC + (LC - k3) % LC
        for k1, pair in enumerate(complex_dft6(re, im)):
            put(k1 * 24 + k2 * LC + k3, pair[0], pair[1])
            put((LA - k1) % LA * 24 + there, pair[0], -pair[1])

    def third_one(k2, carry):
        outer_complex(12 + 2 * k2, k2, 1)
        return carry

    lax.fori_loop(0, LA, third_one, 0)

    def third_even(i, carry):
        outer_complex(6 * (i // 2) + 2 + 2 * (i % 2), 1 + i % 2, 2 * (i // 2))
        return carry

    lax.fori_loop(0, 4, third_even, 0)

    def all_real(i, carry):
        k2, k3 = 3 * (i % 2), 2 * (i // 2)
        slot = 6 * (i // 2) + i % 2
        x0, x3, x1, x2 = real_dft6([stage[r1, slot] for r1 in range(LA)])
        base = k2 * LC + k3
        none = jnp.zeros_like(x0)
        put(base, x0, none)
        put(24 + base, x1[0], x1[1])
        put(48 + base, x2[0], x2[1])
        put(72 + base, x3, none)
        put(96 + base, x2[0], -x2[1])
        put(120 + base, x1[0], -x1[1])
        return carry

    lax.fori_loop(0, 4, all_real, 0)


def placing_tables():
    row = lax.broadcasted_iota(jnp.int32, (256, 256), 0)
    lane = lax.broadcasted_iota(jnp.int32, (256, 256), 1)
    j = ((row >> 4) & 1) * 64 + (row >> 5) * 8 + ((row >> 3) & 1) * 4 + (row & 3)
    part = (row >> 2) & 1
    first = jnp.where(lane == part * 128 + j, 1.0, 0.0)
    sign = jnp.where(part == 0, -1.0, 1.0)
    second = jnp.where(lane == (1 - part) * 128 + j, sign, 0.0)
    return first.astype(BF), second.astype(BF)


def kernel(
    green, screened, panel, column, out,
    g_buf, w_buf, product, cells, stage, spectral, sigma, pan, cols, placing, lhs, to_send, received, quarter,
    to_owner, from_all, final,
    load_sem, col_local, col_send, col_recv, p1_send, p1_recv, p2_send, p2_recv, r_send, r_recv, l_send, l_recv, f_send, f_recv, s_send, s_recv,
):
    ka = lax.axis_index("ka")
    ta = lax.axis_index("ta")
    y, xh = ka // 2, ka % 2
    xl, z, core = ta // (2 * NZ), ta // 2 % NZ, ta % 2
    x = 2 * xh + xl

    def device(y_, x_, z_, core_):
        return (y_ * 2 + x_ // 2, (x_ % 2 * NZ + z_) * 2 + core_)

    barrier = pltpu.get_barrier_semaphore()

    def greet(there):
        pl.semaphore_signal(barrier, inc=1, device_id=there, device_id_type=MESH)

    for dy, dx in FAR_FIRST:
        greet(device((y + dy) % NY, (x + dx) % NX, z, core))
    for dy in (2, 1, 3, 0):
        for dx in (1, 3):
            greet(device((y + dy) % NY, (x + dx) % NX, z, 1 - core))
    greet(device(y, x, z, 1 - core))
    for dz in (4, 3, 5, 2, 6, 1, 7):
        greet(device(y, x, (z + dz) % NZ, core))

    loads = [
        pltpu.make_async_copy(green, g_buf, load_sem.at[0]),
        pltpu.make_async_copy(screened, w_buf, load_sem.at[1]),
        pltpu.make_async_copy(panel.at[:, pl.ds(KH * xl, KH)], pan, load_sem.at[2]),
        pltpu.make_async_copy(column.at[:, pl.ds(KH * xl, KH)], cols.at[0, core], col_local),
    ]
    for load in loads:
        load.start()

    loads[0].wait()
    loads[1].wait()

    def multiply(r, carry):
        for t in range(2):
            product[t, r] = (g_buf[t, r].astype(F32) * w_buf[t, r].astype(F32)).astype(BF)
        return carry

    lax.fori_loop(0, KB, multiply, 0)
    pl.semaphore_wait(barrier, (NZ - 1) + 15 + 8 + 1)

    for dy in (2, 1, 3, 0):
        for t in range(2):
            y_ = (y + dy) % NY
            pltpu.make_async_remote_copy(
                src_ref=product.at[t, :, pl.ds(pl.multiple_of(y_ * SUB, SUB), SUB)],
                dst_ref=cells.at[pl.ds(ka * KB, KB)],
                send_sem=p1_send,
                recv_sem=p1_recv,
                device_id=device(y_, 2 * ((core + t) % 2) + 1 - xl, z, t),
                device_id_type=MESH,
            ).start()

    to_core = pltpu.make_async_remote_copy(
        src_ref=column.at[:, pl.ds(KH * xl, KH)],
        dst_ref=cols.at[0, core],
        send_sem=col_send.at[0],
        recv_sem=col_recv.at[0],
        device_id=device(y, x, z, 1 - core),
        device_id_type=MESH,
    )
    to_x = pltpu.make_async_remote_copy(
        src_ref=column.at[:, pl.ds(KH * (1 - xl), KH)],
        dst_ref=cols.at[1, core],
        send_sem=col_send.at[1],
        recv_sem=col_recv.at[1],
        device_id=device(y, 2 * xh + 1 - xl, z, core),
        device_id_type=MESH,
    )
    forward = pltpu.make_async_remote_copy(
        src_ref=cols.at[1, core],
        dst_ref=cols.at[1, core],
        send_sem=col_send.at[2],
        recv_sem=col_recv.at[2],
        device_id=device(y, x, z, 1 - core),
        device_id_type=MESH,
    )
    to_core.start()

    first, second = placing_tables()
    placing[0:256] = first
    placing[256:512] = second

    def place(side, k):
        parts = [jnp.concatenate([cols[side, b, part, k] for b in range(2)], axis=0) for part in range(2)]
        both = jnp.concatenate(parts, axis=1)
        placed = lax.dot_general(
            placing[...], both, (((1,), (1,)), ((), ())), preferred_element_type=F32
        ).astype(BF)
        return jnp.concatenate([placed[0:256], placed[256:512]], axis=1)

    loads[3].wait()
    to_core.wait_recv()

    def place_own(k, carry):
        lhs[0, k] = place(0, k)
        return carry

    lax.fori_loop(0, KH, place_own, 0)
    to_x.start()
    loads[2].wait()

    pltpu.make_async_copy(cells, cells, p1_recv).wait()
    lattice_dft(cells, stage, spectral)

    place_of = (xh + core) % 2 * NY + y

    def send_points(chunk):
        start, count = STARTS[chunk], CHUNKS[chunk]
        pltpu.make_async_copy(
            spectral.at[:, pl.ds((ka * 2 + xl) * KH + start, count)], sigma[chunk].at[NA + place_of], p2_recv.at[chunk]
        ).start()
        for dy, dx in FAR_FIRST:
            y_, x_ = (y + dy) % NY, (x + dx) % NX
            pltpu.make_async_remote_copy(
                src_ref=spectral.at[:, pl.ds((y_ * NX + x_) * KH + start, count)],
                dst_ref=sigma[chunk].at[(1 + dx) % 2 * NA + place_of],
                send_sem=p2_send.at[chunk],
                recv_sem=p2_recv.at[chunk],
                device_id=device(y_, x_, z, core),
                device_id_type=MESH,
            ).start()

    for chunk in range(AHEAD):
        send_points(chunk)
        if chunk == AHEAD - 2:
            to_x.wait_recv()
            forward.start()
    forward.wait_recv()

    def band_of(chunk, kk, k):
        points = sigma[chunk]
        s = jnp.concatenate([points[:, part, kk].reshape(256, 128) for part in range(2)], axis=1)
        p_re, p_im = pan[0, k], pan[1, k]
        weights = jnp.concatenate(
            [jnp.concatenate([p_re, -p_im], axis=1), jnp.concatenate([p_im, p_re], axis=1)], axis=0
        )
        half = jnp.dot(s, weights, preferred_element_type=F32).astype(BF)
        stacked = jnp.concatenate(
            [half[0:128, 0:128], half[0:128, 128:256], half[128:256, 0:128], half[128:256, 128:256]], axis=0
        )
        rows = jnp.concatenate([lhs[0, k], place(1, k)], axis=1)
        return jnp.dot(rows, stacked, preferred_element_type=F32)

    def contract(chunk):
        start, count = STARTS[chunk], CHUNKS[chunk]
        for kk in range(count):
            to_send[start + kk] = band_of(chunk, kk, start + kk).astype(BF).reshape(NZ, 32, 128)
        for dz in (4, 3, 5, 2, 6, 1, 7):
            z_ = (z + dz) % NZ
            pltpu.make_async_remote_copy(
                src_ref=to_send.at[pl.ds(start, count), z_],
                dst_ref=received.at[z, pl.ds(start, count)],
                send_sem=r_send,
                recv_sem=r_recv.at[chunk],
                device_id=device(y, x, z_, core),
                device_id_type=MESH,
            ).start()

    def finish(chunk):
        start, count = STARTS[chunk], CHUNKS[chunk]
        some = received.at[pl.ds(0, NZ - 1), pl.ds(start, count)]
        pltpu.make_async_copy(some, some, r_recv.at[chunk]).wait()
        for k in range(start, start + count):
            total = to_send[k, z].astype(F32)
            for d in range(1, NZ):
                total = total + received[(z + d) % NZ, k].astype(F32)
            for g in range(4):
                quarter[g, k] = total[8 * g : 8 * g + 8]

        for d in range(1, 4):
            xl_, core_ = (xl + d // 2) % 2, (core + d % 2) % 2
            pltpu.make_async_remote_copy(
                src_ref=quarter.at[2 * xl_ + core_, pl.ds(start, count)],
                dst_ref=out.at[core, pl.ds(KH * xl + start, count)],
                send_sem=f_send,
                recv_sem=f_recv,
                device_id=device(y, 2 * xh + xl_, z, core_),
                device_id_type=MESH,
            ).start()
        out[core, pl.ds(KH * xl + start, count)] = quarter[2 * xl + core, pl.ds(start, count)]

    for chunk in range(LAST):
        if chunk + AHEAD <= LAST:
            send_points(chunk + AHEAD)
        pltpu.make_async_copy(sigma[chunk], sigma[chunk], p2_recv.at[chunk]).wait()
        contract(chunk)

    pltpu.make_async_copy(sigma[LAST], sigma[LAST], p2_recv.at[LAST]).wait()
    for kk in range(CHUNKS[LAST]):
        to_owner[:, kk] = band_of(LAST, kk, EARLY + kk).astype(BF).reshape(NZ * 2, 16, 128)
    for dz in (4, 3, 5, 2, 6, 1, 7, 0):
        for dx in (1, 0):
            if dz or dx:
                z_, xl_ = (z + dz) % NZ, (xl + dx) % 2
                pltpu.make_async_remote_copy(
                    src_ref=to_owner.at[z_ * 2 + xl_],
                    dst_ref=from_all.at[z * 2 + xl],
                    send_sem=l_send,
                    recv_sem=l_recv,
                    device_id=device(y, 2 * xh + xl_, z_, core),
                    device_id_type=MESH,
                ).start()
    from_all[z * 2 + xl] = to_owner[z * 2 + xl]

    for chunk in range(LAST):
        finish(chunk)

    most = from_all.at[pl.ds(0, 15)]
    pltpu.make_async_copy(most, most, l_recv).wait()
    for xl_ in range(2):
        for kk in range(CHUNKS[LAST]):
            total = from_all[xl_, kk].astype(F32)
            for z_ in range(1, NZ):
                total = total + from_all[2 * z_ + xl_, kk].astype(F32)
            for core_ in range(2):
                final[core_, xl_, kk] = total[8 * core_ : 8 * core_ + 8]
    for xl_ in range(2):
        pltpu.make_async_remote_copy(
            src_ref=final.at[1 - core, xl_],
            dst_ref=out.at[core, pl.ds(KH * xl_ + EARLY, CHUNKS[LAST])],
            send_sem=s_send,
            recv_sem=s_recv,
            device_id=device(y, x, z, 1 - core),
            device_id_type=MESH,
        ).start()
    for xl_ in range(2):
        out[core, pl.ds(KH * xl_ + EARLY, CHUNKS[LAST])] = final[core, xl_]

    three = quarter.at[pl.ds(0, 3)]
    pltpu.make_async_copy(three, three, f_recv).wait()

    pltpu.make_async_copy(cells, cells, p1_send).wait()
    to_core.wait_send()
    to_x.wait_send()
    forward.wait_send()
    for chunk in range(len(CHUNKS)):
        others = sigma[chunk].at[pl.ds(0, NY * NX - 1)]
        pltpu.make_async_copy(others, others, p2_send.at[chunk]).wait()
    others = received.at[pl.ds(0, NZ - 1)]
    pltpu.make_async_copy(others, others, r_send).wait()
    pltpu.make_async_copy(most, most, l_send).wait()
    pltpu.make_async_copy(three, three, f_send).wait()
    pltpu.make_async_copy(final.at[0], final.at[0], s_recv).wait()
    pltpu.make_async_copy(final.at[0], final.at[0], s_send).wait()


def body(green, screened, panel, column):
    dma = pltpu.SemaphoreType.DMA
    bands = pl.pallas_call(
        kernel,
        out_shape=jax.ShapeDtypeStruct((2, KB, 8, 128), F32),
        in_specs=[pl.BlockSpec(memory_space=pltpu.HBM)] * 4,
        out_specs=pl.BlockSpec(memory_space=pltpu.VMEM),
        scratch_shapes=[
            pltpu.VMEM((2, KB, 64, 128), BF),
            pltpu.VMEM((2, KB, 64, 128), BF),
            pltpu.VMEM((2, KB, 64, 128), BF),
            pltpu.VMEM((NK, SUB, 128), BF),
            pltpu.VMEM((LA, 24, SUB, 128), F32),
            pltpu.VMEM((2, NK, SUB, 128), BF),
            tuple(pltpu.VMEM((16, 2, count, SUB, 128), BF) for count in CHUNKS),
            pltpu.VMEM((2, KH, 128, 128), BF),
            pltpu.VMEM((2, 2, 2, KH, 64, 128), BF),
            pltpu.VMEM((512, 256), BF),
            pltpu.VMEM((1, KH, 256, 256), BF),
            pltpu.VMEM((EARLY, NZ, 32, 128), BF),
            pltpu.VMEM((NZ, EARLY, 32, 128), BF),
            pltpu.VMEM((4, EARLY, 8, 128), F32),
            pltpu.VMEM((NZ * 2, CHUNKS[LAST], 16, 128), BF),
            pltpu.VMEM((NZ * 2, CHUNKS[LAST], 16, 128), BF),
            pltpu.VMEM((2, 2, CHUNKS[LAST], 8, 128), F32),
            dma((3,)),
            dma,
            dma((3,)),
            dma((3,)),
            dma,
            dma,
            dma((len(CHUNKS),)),
            dma((len(CHUNKS),)),
            dma,
            dma((LAST,)),
            dma,
            dma,
            dma,
            dma,
            dma,
            dma,
        ],
        compiler_params=pltpu.CompilerParams(
            collective_id=0, has_side_effects=True, vmem_limit_bytes=int(53.5 * 1024) * 1024
        ),
    )(green, screened, panel, column)
    return jnp.transpose(bands.reshape(2, KB, 2, 4, 128), (0, 2, 1, 4, 3))


def solution(mesh):
    return jax.shard_map(
        body,
        mesh=mesh,
        in_specs=(
            P(None, "ka", "ta", None),
            P(None, "ka", "ta", None),
            P(None, "ka", None, None),
            P(None, "ka", "ta", None),
        ),
        out_specs=P(None, None, "ka", None, "ta"),
        check_vma=False,
    )
```

```python
import jax
import jax.numpy as jnp
from jax import lax
from jax.experimental import pallas as pl
from jax.experimental.pallas import tpu as pltpu
from jax.sharding import PartitionSpec as P

MESH = pl.DeviceIdType.MESH
BF = jnp.bfloat16
F32 = jnp.float32
NY, NX, NZ = 4, 4, 8
NA = 8
LA, LC = 6, 4
NK = 144
KB = 18
KH = 9
CHUNKS = (2, 1, 2, 2, 2)
STARTS = tuple(sum(CHUNKS[:i]) for i in range(len(CHUNKS)))
LAST = len(CHUNKS) - 1
EARLY = KH - CHUNKS[LAST]
AHEAD = 3
FAR_FIRST = sorted(
    ((dy, dx) for dy in range(NY) for dx in range(NX) if dy or dx),
    key=lambda d: -min(d[0], NY - d[0]) - min(d[1], NX - d[1]),
)
SUB = 16
HALF_SQRT3 = 0.8660254037844386


def real_dft6(x):
    e0, e1, e2 = x[0] + x[3], x[1] + x[4], x[2] + x[5]
    o0, o1, o2 = x[0] - x[3], x[1] - x[4], x[2] - x[5]
    es = e1 + e2
    od = o1 - o2
    x1 = (o0 + 0.5 * od, -HALF_SQRT3 * (o1 + o2))
    x2 = (e0 - 0.5 * es, -HALF_SQRT3 * (e1 - e2))
    return e0 + es, o0 - od, x1, x2


def complex_dft6(re, im):
    a0, a3, a1, a2 = real_dft6(re)
    b0, b3, b1, b2 = real_dft6(im)
    return (
        (a0, b0),
        (a1[0] - b1[1], a1[1] + b1[0]),
        (a2[0] - b2[1], a2[1] + b2[0]),
        (a3, b3),
        (a2[0] + b2[1], b2[0] - a2[1]),
        (a1[0] + b1[1], b1[0] - a1[1]),
    )


def lattice_dft(cells, stage, spectral):
    def inner(r1, carry):
        block = cells[pl.ds(r1 * 24, 24)].astype(F32)
        zero, two, one_re, one_im = [], [], [], []
        for r2 in range(LA):
            x0, x1, x2, x3 = (block[4 * r2 + j] for j in range(LC))
            s02, s13 = x0 + x2, x1 + x3
            zero.append(s02 + s13)
            two.append(s02 - s13)
            one_re.append(x0 - x2)
            one_im.append(x3 - x1)
        for base, values in ((0, zero), (6, two)):
            v0, v3, v1, v2 = real_dft6(values)
            for slot, value in enumerate((v0, v3, v1[0], v1[1], v2[0], v2[1])):
                stage[r1, base + slot] = value
        for k2, pair in enumerate(complex_dft6(one_re, one_im)):
            stage[r1, 12 + 2 * k2] = pair[0]
            stage[r1, 13 + 2 * k2] = pair[1]
        return carry

    lax.fori_loop(0, LA, inner, 0)

    def put(k, re, im):
        spectral[0, k] = re.astype(BF)
        spectral[1, k] = im.astype(BF)

    def outer_complex(slot, k2, k3):
        re = [stage[r1, slot] for r1 in range(LA)]
        im = [stage[r1, slot + 1] for r1 in range(LA)]
        there = (LA - k2) % LA * LC + (LC - k3) % LC
        for k1, pair in enumerate(complex_dft6(re, im)):
            put(k1 * 24 + k2 * LC + k3, pair[0], pair[1])
            put((LA - k1) % LA * 24 + there, pair[0], -pair[1])

    def third_one(k2, carry):
        outer_complex(12 + 2 * k2, k2, 1)
        return carry

    lax.fori_loop(0, LA, third_one, 0)

    def third_even(i, carry):
        outer_complex(6 * (i // 2) + 2 + 2 * (i % 2), 1 + i % 2, 2 * (i // 2))
        return carry

    lax.fori_loop(0, 4, third_even, 0)

    def all_real(i, carry):
        k2, k3 = 3 * (i % 2), 2 * (i // 2)
        slot = 6 * (i // 2) + i % 2
        x0, x3, x1, x2 = real_dft6([stage[r1, slot] for r1 in range(LA)])
        base = k2 * LC + k3
        none = jnp.zeros_like(x0)
        put(base, x0, none)
        put(24 + base, x1[0], x1[1])
        put(48 + base, x2[0], x2[1])
        put(72 + base, x3, none)
        put(96 + base, x2[0], -x2[1])
        put(120 + base, x1[0], -x1[1])
        return carry

    lax.fori_loop(0, 4, all_real, 0)


def placing_tables():
    row = lax.broadcasted_iota(jnp.int32, (256, 256), 0)
    lane = lax.broadcasted_iota(jnp.int32, (256, 256), 1)
    j = ((row >> 4) & 1) * 64 + (row >> 5) * 8 + ((row >> 3) & 1) * 4 + (row & 3)
    part = (row >> 2) & 1
    first = jnp.where(lane == part * 128 + j, 1.0, 0.0)
    sign = jnp.where(part == 0, -1.0, 1.0)
    second = jnp.where(lane == (1 - part) * 128 + j, sign, 0.0)
    return first.astype(BF), second.astype(BF)


def kernel(
    green, screened, panel, column, out,
    g_buf, w_buf, product, cells, stage, spectral, sigma, pan, cols, placing, lhs, to_send, received, quarter,
    to_owner, from_all, final,
    load_sem, col_local, col_send, col_recv, p1_send, p1_recv, p2_send, p2_recv, r_send, r_recv, l_send, l_recv, f_send, f_recv, s_send, s_recv,
):
    ka = lax.axis_index("ka")
    ta = lax.axis_index("ta")
    y, xh = ka // 2, ka % 2
    xl, z, core = ta // (2 * NZ), ta // 2 % NZ, ta % 2
    x = 2 * xh + xl

    def device(y_, x_, z_, core_):
        return (y_ * 2 + x_ // 2, (x_ % 2 * NZ + z_) * 2 + core_)

    barrier = pltpu.get_barrier_semaphore()

    def greet(there):
        pl.semaphore_signal(barrier, inc=1, device_id=there, device_id_type=MESH)

    for dy, dx in FAR_FIRST:
        greet(device((y + dy) % NY, (x + dx) % NX, z, core))
    for dy in (2, 1, 3, 0):
        for dx in (1, 3):
            greet(device((y + dy) % NY, (x + dx) % NX, z, 1 - core))
    greet(device(y, x, z, 1 - core))
    for dz in (4, 3, 5, 2, 6, 1, 7):
        greet(device(y, x, (z + dz) % NZ, core))

    loads = [
        pltpu.make_async_copy(green, g_buf, load_sem.at[0]),
        pltpu.make_async_copy(screened, w_buf, load_sem.at[1]),
        pltpu.make_async_copy(panel.at[:, pl.ds(KH * xl, KH)], pan, load_sem.at[2]),
        pltpu.make_async_copy(column.at[:, pl.ds(KH * xl, KH)], cols.at[0, core], col_local),
    ]
    for load in loads:
        load.start()

    loads[0].wait()
    loads[1].wait()

    def multiply(r, carry):
        for t in range(2):
            product[t, r] = (g_buf[t, r].astype(F32) * w_buf[t, r].astype(F32)).astype(BF)
        return carry

    lax.fori_loop(0, KB, multiply, 0)
    pl.semaphore_wait(barrier, (NZ - 1) + 15 + 8 + 1)

    for dy in (2, 1, 3, 0):
        for t in range(2):
            y_ = (y + dy) % NY
            pltpu.make_async_remote_copy(
                src_ref=product.at[t, :, pl.ds(pl.multiple_of(y_ * SUB, SUB), SUB)],
                dst_ref=cells.at[pl.ds(ka * KB, KB)],
                send_sem=p1_send,
                recv_sem=p1_recv,
                device_id=device(y_, 2 * ((core + t) % 2) + 1 - xl, z, t),
                device_id_type=MESH,
            ).start()

    to_core = pltpu.make_async_remote_copy(
        src_ref=column.at[:, pl.ds(KH * xl, KH)],
        dst_ref=cols.at[0, core],
        send_sem=col_send.at[0],
        recv_sem=col_recv.at[0],
        device_id=device(y, x, z, 1 - core),
        device_id_type=MESH,
    )
    to_x = pltpu.make_async_remote_copy(
        src_ref=column.at[:, pl.ds(KH * (1 - xl), KH)],
        dst_ref=cols.at[1, core],
        send_sem=col_send.at[1],
        recv_sem=col_recv.at[1],
        device_id=device(y, 2 * xh + 1 - xl, z, core),
        device_id_type=MESH,
    )
    forward = pltpu.make_async_remote_copy(
        src_ref=cols.at[1, core],
        dst_ref=cols.at[1, core],
        send_sem=col_send.at[2],
        recv_sem=col_recv.at[2],
        device_id=device(y, x, z, 1 - core),
        device_id_type=MESH,
    )
    to_core.start()

    first, second = placing_tables()
    placing[0:256] = first
    placing[256:512] = second

    def place(side, k):
        parts = [jnp.concatenate([cols[side, b, part, k] for b in range(2)], axis=0) for part in range(2)]
        both = jnp.concatenate(parts, axis=1)
        placed = lax.dot_general(
            placing[...], both, (((1,), (1,)), ((), ())), preferred_element_type=F32
        ).astype(BF)
        return jnp.concatenate([placed[0:256], placed[256:512]], axis=1)

    loads[3].wait()
    to_core.wait_recv()

    def place_own(k, carry):
        lhs[0, k] = place(0, k)
        return carry

    lax.fori_loop(0, KH, place_own, 0)
    to_x.start()
    loads[2].wait()

    pltpu.make_async_copy(cells, cells, p1_recv).wait()
    lattice_dft(cells, stage, spectral)

    place_of = (xh + core) % 2 * NY + y

    def send_points(chunk):
        start, count = STARTS[chunk], CHUNKS[chunk]
        pltpu.make_async_copy(
            spectral.at[:, pl.ds((ka * 2 + xl) * KH + start, count)], sigma[chunk].at[NA + place_of], p2_recv.at[chunk]
        ).start()
        for dy, dx in FAR_FIRST:
            y_, x_ = (y + dy) % NY, (x + dx) % NX
            pltpu.make_async_remote_copy(
                src_ref=spectral.at[:, pl.ds((y_ * NX + x_) * KH + start, count)],
                dst_ref=sigma[chunk].at[(1 + dx) % 2 * NA + place_of],
                send_sem=p2_send.at[chunk],
                recv_sem=p2_recv.at[chunk],
                device_id=device(y_, x_, z, core),
                device_id_type=MESH,
            ).start()

    for chunk in range(AHEAD):
        send_points(chunk)
        if chunk == AHEAD - 2:
            to_x.wait_recv()
            forward.start()
    forward.wait_recv()

    def band_of(chunk, kk, k):
        points = sigma[chunk]
        s = jnp.concatenate([points[:, part, kk].reshape(256, 128) for part in range(2)], axis=1)
        p_re, p_im = pan[0, k], pan[1, k]
        weights = jnp.concatenate(
            [jnp.concatenate([p_re, -p_im], axis=1), jnp.concatenate([p_im, p_re], axis=1)], axis=0
        )
        half = jnp.dot(s, weights, preferred_element_type=F32).astype(BF)
        stacked = jnp.concatenate(
            [half[0:128, 0:128], half[0:128, 128:256], half[128:256, 0:128], half[128:256, 128:256]], axis=0
        )
        rows = jnp.concatenate([lhs[0, k], place(1, k)], axis=1)
        return jnp.dot(rows, stacked, preferred_element_type=F32)

    def contract(chunk):
        start, count = STARTS[chunk], CHUNKS[chunk]
        for kk in range(count):
            to_send[start + kk] = band_of(chunk, kk, start + kk).astype(BF).reshape(NZ, 32, 128)
        for dz in (4, 3, 5, 2, 6, 1, 7):
            z_ = (z + dz) % NZ
            pltpu.make_async_remote_copy(
                src_ref=to_send.at[pl.ds(start, count), z_],
                dst_ref=received.at[z, pl.ds(start, count)],
                send_sem=r_send,
                recv_sem=r_recv.at[chunk],
                device_id=device(y, x, z_, core),
                device_id_type=MESH,
            ).start()

    def finish(chunk):
        start, count = STARTS[chunk], CHUNKS[chunk]
        some = received.at[pl.ds(0, NZ - 1), pl.ds(start, count)]
        pltpu.make_async_copy(some, some, r_recv.at[chunk]).wait()
        for k in range(start, start + count):
            total = to_send[k, z].astype(F32)
            for d in range(1, NZ):
                total = total + received[(z + d) % NZ, k].astype(F32)
            for g in range(4):
                quarter[g, k] = total[8 * g : 8 * g + 8]

        for d in range(1, 4):
            xl_, core_ = (xl + d // 2) % 2, (core + d % 2) % 2
            pltpu.make_async_remote_copy(
                src_ref=quarter.at[2 * xl_ + core_, pl.ds(start, count)],
                dst_ref=out.at[core, pl.ds(KH * xl + start, count)],
                send_sem=f_send,
                recv_sem=f_recv,
                device_id=device(y, 2 * xh + xl_, z, core_),
                device_id_type=MESH,
            ).start()
        out[core, pl.ds(KH * xl + start, count)] = quarter[2 * xl + core, pl.ds(start, count)]

    for chunk in range(LAST):
        if chunk + AHEAD <= LAST:
            send_points(chunk + AHEAD)
        pltpu.make_async_copy(sigma[chunk], sigma[chunk], p2_recv.at[chunk]).wait()
        contract(chunk)

    pltpu.make_async_copy(sigma[LAST], sigma[LAST], p2_recv.at[LAST]).wait()
    for kk in range(CHUNKS[LAST]):
        to_owner[:, kk] = band_of(LAST, kk, EARLY + kk).astype(BF).reshape(NZ * 2, 16, 128)
    for dz in (4, 3, 5, 2, 6, 1, 7, 0):
        for dx in (1, 0):
            if dz or dx:
                z_, xl_ = (z + dz) % NZ, (xl + dx) % 2
                pltpu.make_async_remote_copy(
                    src_ref=to_owner.at[z_ * 2 + xl_],
                    dst_ref=from_all.at[z * 2 + xl],
                    send_sem=l_send,
                    recv_sem=l_recv,
                    device_id=device(y, 2 * xh + xl_, z_, core),
                    device_id_type=MESH,
                ).start()
    from_all[z * 2 + xl] = to_owner[z * 2 + xl]

    for chunk in range(LAST):
        finish(chunk)

    most = from_all.at[pl.ds(0, 15)]
    pltpu.make_async_copy(cells, cells, p1_send).wait()
    to_core.wait_send()
    to_x.wait_send()
    forward.wait_send()
    for chunk in range(len(CHUNKS)):
        others = sigma[chunk].at[pl.ds(0, NY * NX - 1)]
        pltpu.make_async_copy(others, others, p2_send.at[chunk]).wait()
    others = received.at[pl.ds(0, NZ - 1)]
    pltpu.make_async_copy(others, others, r_send).wait()
    pltpu.make_async_copy(most, most, l_send).wait()

    pltpu.make_async_copy(most, most, l_recv).wait()
    for xl_ in range(2):
        for kk in range(CHUNKS[LAST]):
            total = from_all[xl_, kk].astype(F32)
            for z_ in range(1, NZ):
                total = total + from_all[2 * z_ + xl_, kk].astype(F32)
            for core_ in range(2):
                final[core_, xl_, kk] = total[8 * core_ : 8 * core_ + 8]
    for xl_ in range(2):
        pltpu.make_async_remote_copy(
            src_ref=final.at[1 - core, xl_],
            dst_ref=out.at[core, pl.ds(KH * xl_ + EARLY, CHUNKS[LAST])],
            send_sem=s_send,
            recv_sem=s_recv,
            device_id=device(y, x, z, 1 - core),
            device_id_type=MESH,
        ).start()
    for xl_ in range(2):
        out[core, pl.ds(KH * xl_ + EARLY, CHUNKS[LAST])] = final[core, xl_]

    three = quarter.at[pl.ds(0, 3)]
    pltpu.make_async_copy(three, three, f_recv).wait()

    pltpu.make_async_copy(three, three, f_send).wait()
    pltpu.make_async_copy(final.at[0], final.at[0], s_recv).wait()
    pltpu.make_async_copy(final.at[0], final.at[0], s_send).wait()


def body(green, screened, panel, column):
    dma = pltpu.SemaphoreType.DMA
    bands = pl.pallas_call(
        kernel,
        out_shape=jax.ShapeDtypeStruct((2, KB, 8, 128), F32),
        in_specs=[pl.BlockSpec(memory_space=pltpu.HBM)] * 4,
        out_specs=pl.BlockSpec(memory_space=pltpu.VMEM),
        scratch_shapes=[
            pltpu.VMEM((2, KB, 64, 128), BF),
            pltpu.VMEM((2, KB, 64, 128), BF),
            pltpu.VMEM((2, KB, 64, 128), BF),
            pltpu.VMEM((NK, SUB, 128), BF),
            pltpu.VMEM((LA, 24, SUB, 128), F32),
            pltpu.VMEM((2, NK, SUB, 128), BF),
            tuple(pltpu.VMEM((16, 2, count, SUB, 128), BF) for count in CHUNKS),
            pltpu.VMEM((2, KH, 128, 128), BF),
            pltpu.VMEM((2, 2, 2, KH, 64, 128), BF),
            pltpu.VMEM((512, 256), BF),
            pltpu.VMEM((1, KH, 256, 256), BF),
            pltpu.VMEM((EARLY, NZ, 32, 128), BF),
            pltpu.VMEM((NZ, EARLY, 32, 128), BF),
            pltpu.VMEM((4, EARLY, 8, 128), F32),
            pltpu.VMEM((NZ * 2, CHUNKS[LAST], 16, 128), BF),
            pltpu.VMEM((NZ * 2, CHUNKS[LAST], 16, 128), BF),
            pltpu.VMEM((2, 2, CHUNKS[LAST], 8, 128), F32),
            dma((3,)),
            dma,
            dma((3,)),
            dma((3,)),
            dma,
            dma,
            dma((len(CHUNKS),)),
            dma((len(CHUNKS),)),
            dma,
            dma((LAST,)),
            dma,
            dma,
            dma,
            dma,
            dma,
            dma,
        ],
        compiler_params=pltpu.CompilerParams(
            collective_id=0, has_side_effects=True, vmem_limit_bytes=int(53.5 * 1024) * 1024
        ),
    )(green, screened, panel, column)
    return jnp.transpose(bands.reshape(2, KB, 2, 4, 128), (0, 2, 1, 4, 3))


def solution(mesh):
    return jax.shard_map(
        body,
        mesh=mesh,
        in_specs=(
            P(None, "ka", "ta", None),
            P(None, "ka", "ta", None),
            P(None, "ka", None, None),
            P(None, "ka", "ta", None),
        ),
        out_specs=P(None, None, "ka", None, "ta"),
        check_vma=False,
    )
```

```python
import jax
import jax.numpy as jnp
from jax import lax
from jax.experimental import pallas as pl
from jax.experimental.pallas import tpu as pltpu
from jax.sharding import PartitionSpec as P

MESH = pl.DeviceIdType.MESH
BF = jnp.bfloat16
F32 = jnp.float32
NY, NX, NZ = 4, 4, 8
NA = 8
LA, LC = 6, 4
NK = 144
KB = 18
KH = 9
CHUNKS = (2, 1, 2, 2, 2)
STARTS = tuple(sum(CHUNKS[:i]) for i in range(len(CHUNKS)))
LAST = len(CHUNKS) - 1
EARLY = KH - CHUNKS[LAST]
SHY = 1
PARTNER_LAST = [(dy, dx) for dx in (0, 1, 2, 3) for dy in (2, 1, 3, 0) if dy or dx]
AHEAD = 3
FAR_FIRST = sorted(
    ((dy, dx) for dy in range(NY) for dx in range(NX) if dy or dx),
    key=lambda d: -min(d[0], NY - d[0]) - min(d[1], NX - d[1]),
)
SUB = 16
HALF_SQRT3 = 0.8660254037844386


def real_dft6(x):
    e0, e1, e2 = x[0] + x[3], x[1] + x[4], x[2] + x[5]
    o0, o1, o2 = x[0] - x[3], x[1] - x[4], x[2] - x[5]
    es = e1 + e2
    od = o1 - o2
    x1 = (o0 + 0.5 * od, -HALF_SQRT3 * (o1 + o2))
    x2 = (e0 - 0.5 * es, -HALF_SQRT3 * (e1 - e2))
    return e0 + es, o0 - od, x1, x2


def complex_dft6(re, im):
    a0, a3, a1, a2 = real_dft6(re)
    b0, b3, b1, b2 = real_dft6(im)
    return (
        (a0, b0),
        (a1[0] - b1[1], a1[1] + b1[0]),
        (a2[0] - b2[1], a2[1] + b2[0]),
        (a3, b3),
        (a2[0] + b2[1], b2[0] - a2[1]),
        (a1[0] + b1[1], b1[0] - a1[1]),
    )


def lattice_dft(cells, stage, spectral):
    def inner(r1, carry):
        block = cells[pl.ds(r1 * 24, 24)].astype(F32)
        zero, two, one_re, one_im = [], [], [], []
        for r2 in range(LA):
            x0, x1, x2, x3 = (block[4 * r2 + j] for j in range(LC))
            s02, s13 = x0 + x2, x1 + x3
            zero.append(s02 + s13)
            two.append(s02 - s13)
            one_re.append(x0 - x2)
            one_im.append(x3 - x1)
        for base, values in ((0, zero), (6, two)):
            v0, v3, v1, v2 = real_dft6(values)
            for slot, value in enumerate((v0, v3, v1[0], v1[1], v2[0], v2[1])):
                stage[r1, base + slot] = value
        for k2, pair in enumerate(complex_dft6(one_re, one_im)):
            stage[r1, 12 + 2 * k2] = pair[0]
            stage[r1, 13 + 2 * k2] = pair[1]
        return carry

    lax.fori_loop(0, LA, inner, 0)

    def put(k, re, im):
        spectral[k, 0] = re.astype(BF)
        spectral[k, 1] = im.astype(BF)

    def outer_complex(slot, k2, k3):
        re = [stage[r1, slot] for r1 in range(LA)]
        im = [stage[r1, slot + 1] for r1 in range(LA)]
        there = (LA - k2) % LA * LC + (LC - k3) % LC
        for k1, pair in enumerate(complex_dft6(re, im)):
            put(k1 * 24 + k2 * LC + k3, pair[0], pair[1])
            put((LA - k1) % LA * 24 + there, pair[0], -pair[1])

    def third_one(k2, carry):
        outer_complex(12 + 2 * k2, k2, 1)
        return carry

    lax.fori_loop(0, LA, third_one, 0)

    def third_even(i, carry):
        outer_complex(6 * (i // 2) + 2 + 2 * (i % 2), 1 + i % 2, 2 * (i // 2))
        return carry

    lax.fori_loop(0, 4, third_even, 0)

    def all_real(i, carry):
        k2, k3 = 3 * (i % 2), 2 * (i // 2)
        slot = 6 * (i // 2) + i % 2
        x0, x3, x1, x2 = real_dft6([stage[r1, slot] for r1 in range(LA)])
        base = k2 * LC + k3
        none = jnp.zeros_like(x0)
        put(base, x0, none)
        put(24 + base, x1[0], x1[1])
        put(48 + base, x2[0], x2[1])
        put(72 + base, x3, none)
        put(96 + base, x2[0], -x2[1])
        put(120 + base, x1[0], -x1[1])
        return carry

    lax.fori_loop(0, 4, all_real, 0)


def placing_tables():
    row = lax.broadcasted_iota(jnp.int32, (256, 256), 0)
    lane = lax.broadcasted_iota(jnp.int32, (256, 256), 1)
    j = ((row >> 4) & 1) * 64 + (row >> 5) * 8 + ((row >> 3) & 1) * 4 + (row & 3)
    part = (row >> 2) & 1
    first = jnp.where(lane == part * 128 + j, 1.0, 0.0)
    sign = jnp.where(part == 0, -1.0, 1.0)
    second = jnp.where(lane == (1 - part) * 128 + j, sign, 0.0)
    return first.astype(BF), second.astype(BF)


def kernel(
    green, screened, panel, column, out,
    g_buf, w_buf, product, cells, stage, spectral, sigma, pan, cols, placing, lhs, to_send, received, quarter,
    to_owner, from_all, final,
    load_sem, col_local, col_send, col_recv, p1_send, p1_recv, p2_send, p2_recv, r_send, r_recv, l_send, l_recv, f_send, f_recv, s_send, s_recv,
):
    ka = lax.axis_index("ka")
    ta = lax.axis_index("ta")
    y, xh = ka // 2, ka % 2
    xl, z, core = ta // (2 * NZ), ta // 2 % NZ, ta % 2
    x = 2 * xh + xl

    def device(y_, x_, z_, core_):
        return (y_ * 2 + x_ // 2, (x_ % 2 * NZ + z_) * 2 + core_)

    loads = [
        pltpu.make_async_copy(green, g_buf, load_sem.at[0]),
        pltpu.make_async_copy(screened, w_buf, load_sem.at[1]),
        pltpu.make_async_copy(panel.at[:, pl.ds(KH * xl, KH)], pan, load_sem.at[2]),
        pltpu.make_async_copy(column.at[:, pl.ds(KH * xl, KH)], cols.at[0, core], col_local),
    ]
    loads[0].start()
    loads[1].start()

    barrier = pltpu.get_barrier_semaphore()

    def greet(there):
        pl.semaphore_signal(barrier, inc=1, device_id=there, device_id_type=MESH)

    for dy, dx in FAR_FIRST:
        greet(device((y + dy) % NY, (x + dx) % NX, z, core))
    for dy in (2, 1, 3, 0):
        for dx in (1, 3):
            greet(device((y + dy) % NY, (x + dx) % NX, z, 1 - core))
    greet(device(y, x, z, 1 - core))
    for dz in (4, 3, 5, 2, 6, 1, 7):
        greet(device(y, x, (z + dz) % NZ, core))

    loads[2].start()
    loads[3].start()
    loads[0].wait()
    loads[1].wait()

    def multiply(r, carry):
        for t in range(2):
            both = g_buf[t, r].astype(F32) * w_buf[t, r].astype(F32)
            product[t, :, r] = both.astype(BF).reshape(NY, SUB, 128)
        return carry

    lax.fori_loop(0, KB, multiply, 0)
    pl.semaphore_wait(barrier, (NZ - 1) + 15 + 8 + 1)

    for dy in (2, 1, 3, 0):
        for t in range(2):
            y_ = (y + dy) % NY
            pltpu.make_async_remote_copy(
                src_ref=product.at[t, y_],
                dst_ref=cells.at[pl.ds(ka * KB, KB)],
                send_sem=p1_send,
                recv_sem=p1_recv,
                device_id=device(y_, 2 * ((core + t) % 2) + 1 - xl, z, t),
                device_id_type=MESH,
            ).start()

    to_core = pltpu.make_async_remote_copy(
        src_ref=column.at[:, pl.ds(KH * xl, KH)],
        dst_ref=cols.at[0, core],
        send_sem=col_send.at[0],
        recv_sem=col_recv.at[0],
        device_id=device(y, x, z, 1 - core),
        device_id_type=MESH,
    )
    to_x = pltpu.make_async_remote_copy(
        src_ref=column.at[:, pl.ds(KH * (1 - xl), KH)],
        dst_ref=cols.at[1, core],
        send_sem=col_send.at[1],
        recv_sem=col_recv.at[1],
        device_id=device(y, 2 * xh + 1 - xl, z, core),
        device_id_type=MESH,
    )
    forward = pltpu.make_async_remote_copy(
        src_ref=cols.at[1, core],
        dst_ref=cols.at[1, core],
        send_sem=col_send.at[2],
        recv_sem=col_recv.at[2],
        device_id=device(y, x, z, 1 - core),
        device_id_type=MESH,
    )
    to_core.start()

    first, second = placing_tables()
    placing[0:256] = first
    placing[256:512] = second

    def place(side, k):
        parts = [jnp.concatenate([cols[side, b, part, k] for b in range(2)], axis=0) for part in range(2)]
        both = jnp.concatenate(parts, axis=1)
        placed = lax.dot_general(
            placing[...], both, (((1,), (1,)), ((), ())), preferred_element_type=F32
        ).astype(BF)
        return jnp.concatenate([placed[0:256], placed[256:512]], axis=1)

    loads[3].wait()
    to_core.wait_recv()

    to_x.start()

    def place_own(k, carry):
        lhs[0, k] = place(0, k)
        return carry

    lax.fori_loop(0, KH, place_own, 0)
    loads[2].wait()

    pltpu.make_async_copy(cells, cells, p1_recv).wait()
    lattice_dft(cells, stage, spectral)

    place_of = (xh + core) % 2 * NY + y

    def send_points(chunk):
        start, count = STARTS[chunk], CHUNKS[chunk]
        pltpu.make_async_copy(
            spectral.at[pl.ds((ka * 2 + xl) * KH + start, count)], sigma[chunk].at[NA + place_of], p2_recv.at[chunk]
        ).start()
        for dy, dx in PARTNER_LAST if chunk < SHY else FAR_FIRST:
            y_ = (y + dy) % NY
            x_ = (x + (NX - dx + 2 * dx * xl if chunk < SHY else dx)) % NX
            pltpu.make_async_remote_copy(
                src_ref=spectral.at[pl.ds((y_ * NX + x_) * KH + start, count)],
                dst_ref=sigma[chunk].at[(1 + dx) % 2 * NA + place_of],
                send_sem=p2_send.at[chunk],
                recv_sem=p2_recv.at[chunk],
                device_id=device(y_, x_, z, core),
                device_id_type=MESH,
            ).start()

    for chunk in range(AHEAD):
        send_points(chunk)
        if chunk == AHEAD - 2:
            to_x.wait_recv()
            forward.start()
    forward.wait_recv()

    def band_of(chunk, kk, k):
        points = sigma[chunk]
        s = jnp.concatenate([points[:, kk, part].reshape(256, 128) for part in range(2)], axis=1)
        p_re, p_im = pan[0, k], pan[1, k]
        weights = jnp.concatenate(
            [jnp.concatenate([p_re, -p_im], axis=1), jnp.concatenate([p_im, p_re], axis=1)], axis=0
        )
        half = jnp.dot(s, weights, preferred_element_type=F32).astype(BF)
        stacked = jnp.concatenate(
            [half[0:128, 0:128], half[0:128, 128:256], half[128:256, 0:128], half[128:256, 128:256]], axis=0
        )
        other = lhs[1, k] if chunk == LAST else place(1, k)
        rows = jnp.concatenate([lhs[0, k], other], axis=1)
        return jnp.dot(rows, stacked, preferred_element_type=F32)

    def contract(chunk):
        start, count = STARTS[chunk], CHUNKS[chunk]
        for kk in range(count):
            to_send[start + kk] = band_of(chunk, kk, start + kk).astype(BF).reshape(NZ, 32, 128)
        for dz in (4, 3, 5, 2, 6, 1, 7):
            z_ = (z + dz) % NZ
            pltpu.make_async_remote_copy(
                src_ref=to_send.at[pl.ds(start, count), z_],
                dst_ref=received.at[z, pl.ds(start, count)],
                send_sem=r_send,
                recv_sem=r_recv.at[chunk],
                device_id=device(y, x, z_, core),
                device_id_type=MESH,
            ).start()

    def finish(chunk):
        start, count = STARTS[chunk], CHUNKS[chunk]
        some = received.at[pl.ds(0, NZ - 1), pl.ds(start, count)]
        pltpu.make_async_copy(some, some, r_recv.at[chunk]).wait()
        for k in range(start, start + count):
            total = to_send[k, z].astype(F32)
            for d in range(1, NZ):
                total = total + received[(z + d) % NZ, k].astype(F32)
            for g in range(4):
                quarter[g, k] = total[8 * g : 8 * g + 8]

        for d in range(1, 4):
            xl_, core_ = (xl + d // 2) % 2, (core + d % 2) % 2
            pltpu.make_async_remote_copy(
                src_ref=quarter.at[2 * xl_ + core_, pl.ds(start, count)],
                dst_ref=out.at[core, pl.ds(KH * xl + start, count)],
                send_sem=f_send,
                recv_sem=f_recv,
                device_id=device(y, 2 * xh + xl_, z, core_),
                device_id_type=MESH,
            ).start()
        out[core, pl.ds(KH * xl + start, count)] = quarter[2 * xl + core, pl.ds(start, count)]

    for chunk in range(LAST):
        if chunk + AHEAD <= LAST:
            send_points(chunk + AHEAD)
        pltpu.make_async_copy(sigma[chunk], sigma[chunk], p2_recv.at[chunk]).wait()
        contract(chunk)

    for k in range(EARLY, KH):
        lhs[1, k] = place(1, k)
    pltpu.make_async_copy(sigma[LAST], sigma[LAST], p2_recv.at[LAST]).wait()
    for kk in range(CHUNKS[LAST]):
        to_owner[:, kk] = band_of(LAST, kk, EARLY + kk).astype(BF).reshape(NZ * 2, 16, 128)
    for dz in (4, 3, 5, 2, 6, 1, 7, 0):
        for dx in (1, 0):
            if dz or dx:
                z_, xl_ = (z + dz) % NZ, (xl + dx) % 2
                pltpu.make_async_remote_copy(
                    src_ref=to_owner.at[z_ * 2 + xl_],
                    dst_ref=from_all.at[z * 2 + xl],
                    send_sem=l_send,
                    recv_sem=l_recv,
                    device_id=device(y, 2 * xh + xl_, z_, core),
                    device_id_type=MESH,
                ).start()
    from_all[z * 2 + xl] = to_owner[z * 2 + xl]

    for chunk in range(LAST):
        finish(chunk)

    most = from_all.at[pl.ds(0, 15)]
    pltpu.make_async_copy(cells, cells, p1_send).wait()
    to_core.wait_send()
    to_x.wait_send()
    forward.wait_send()
    for chunk in range(len(CHUNKS)):
        others = sigma[chunk].at[pl.ds(0, NY * NX - 1)]
        pltpu.make_async_copy(others, others, p2_send.at[chunk]).wait()
    others = received.at[pl.ds(0, NZ - 1)]
    pltpu.make_async_copy(others, others, r_send).wait()
    pltpu.make_async_copy(most, most, l_send).wait()

    pltpu.make_async_copy(most, most, l_recv).wait()
    for xl_ in range(2):
        for kk in range(CHUNKS[LAST]):
            total = from_all[xl_, kk].astype(F32)
            for z_ in range(1, NZ):
                total = total + from_all[2 * z_ + xl_, kk].astype(F32)
            for core_ in range(2):
                final[core_, xl_, kk] = total[8 * core_ : 8 * core_ + 8]
    for xl_ in range(2):
        pltpu.make_async_remote_copy(
            src_ref=final.at[1 - core, xl_],
            dst_ref=out.at[core, pl.ds(KH * xl_ + EARLY, CHUNKS[LAST])],
            send_sem=s_send,
            recv_sem=s_recv,
            device_id=device(y, x, z, 1 - core),
            device_id_type=MESH,
        ).start()
    for xl_ in range(2):
        out[core, pl.ds(KH * xl_ + EARLY, CHUNKS[LAST])] = final[core, xl_]

    three = quarter.at[pl.ds(0, 3)]
    pltpu.make_async_copy(three, three, f_recv).wait()

    pltpu.make_async_copy(three, three, f_send).wait()
    pltpu.make_async_copy(final.at[0], final.at[0], s_recv).wait()
    pltpu.make_async_copy(final.at[0], final.at[0], s_send).wait()


def body(green, screened, panel, column):
    dma = pltpu.SemaphoreType.DMA
    bands = pl.pallas_call(
        kernel,
        out_shape=jax.ShapeDtypeStruct((2, KB, 8, 128), F32),
        in_specs=[pl.BlockSpec(memory_space=pltpu.HBM)] * 4,
        out_specs=pl.BlockSpec(memory_space=pltpu.VMEM),
        scratch_shapes=[
            pltpu.VMEM((2, KB, 64, 128), BF),
            pltpu.VMEM((2, KB, 64, 128), BF),
            pltpu.VMEM((2, NY, KB, SUB, 128), BF),
            pltpu.VMEM((NK, SUB, 128), BF),
            pltpu.VMEM((LA, 24, SUB, 128), F32),
            pltpu.VMEM((NK, 2, SUB, 128), BF),
            tuple(pltpu.VMEM((16, count, 2, SUB, 128), BF) for count in CHUNKS),
            pltpu.VMEM((2, KH, 128, 128), BF),
            pltpu.VMEM((2, 2, 2, KH, 64, 128), BF),
            pltpu.VMEM((512, 256), BF),
            pltpu.VMEM((2, KH, 256, 256), BF),
            pltpu.VMEM((EARLY, NZ, 32, 128), BF),
            pltpu.VMEM((NZ, EARLY, 32, 128), BF),
            pltpu.VMEM((4, EARLY, 8, 128), F32),
            pltpu.VMEM((NZ * 2, CHUNKS[LAST], 16, 128), BF),
            pltpu.VMEM((NZ * 2, CHUNKS[LAST], 16, 128), BF),
            pltpu.VMEM((2, 2, CHUNKS[LAST], 8, 128), F32),
            dma((3,)),
            dma,
            dma((3,)),
            dma((3,)),
            dma,
            dma,
            dma((len(CHUNKS),)),
            dma((len(CHUNKS),)),
            dma,
            dma((LAST,)),
            dma,
            dma,
            dma,
            dma,
            dma,
            dma,
        ],
        compiler_params=pltpu.CompilerParams(
            collective_id=0, has_side_effects=True, vmem_limit_bytes=int(53.5 * 1024) * 1024
        ),
    )(green, screened, panel, column)
    return jnp.transpose(bands.reshape(2, KB, 2, 4, 128), (0, 2, 1, 4, 3))


def solution(mesh):
    return jax.shard_map(
        body,
        mesh=mesh,
        in_specs=(
            P(None, "ka", "ta", None),
            P(None, "ka", "ta", None),
            P(None, "ka", None, None),
            P(None, "ka", "ta", None),
        ),
        out_specs=P(None, None, "ka", None, "ta"),
        check_vma=False,
    )
```
